512 devices in a mesh: section: 4 (over y), row: 16 (over z), col: 8 (over x, core).
Axes of the slice: x: 4, y: 4, z: 16, core: 2. Of those that a mesh axis runs over, the one named last changes fastest.
Arguments:
- grad_out: bfloat16 [4, 320, 6144], P('section', 'col', 'row'), may hold values from -34 to 34
- pre_act: bfloat16 [4, 320, 24576], P('section', 'row', 'col'), may hold values from -36 to 36
- w_down: bfloat16 [4, 24576, 6144], P('section', 'col', 'row'), may hold values from -0.0390625 to 0.0390625
Outputs:
- grad_pre: bfloat16 [4, 320, 24576], P('section', 'row', 'col')
- grad_weight: bfloat16 [4, 24576, 6144], P('section', 'col', 'row')
The draws below stay inside these ranges and needn't reach their ends.
All inputs are finite; a program needn't handle non-finite values.
Results may differ from the reference program's by a relative error of at most 0.0034.
Values may be sent and summed in bfloat16 or wider, within the bound.
A program may use at most 64 MiB of HBM per device.

```python
import math
import jax
import jax.numpy as jnp
from jax import lax

D = 6144
FFW = 24576
TOK_SECTION = 320
SECTIONS = 4


def draw_grad_out(key, part):
    key = jax.random.fold_in(key, 11)
    key_base, key_jitter = jax.random.split(key, 2)
    shape = (SECTIONS, TOK_SECTION, D)
    columns = (jnp.arange(D, dtype=jnp.float32) + 0.5) / D
    section_pos = jnp.arange(SECTIONS, dtype=jnp.float32) / max(SECTIONS - 1, 1)
    jitter = jax.random.uniform(key_jitter, (D,), jnp.float32, 0.0, 0.25)
    base = jax.random.truncated_normal(key_base, -6.0, 6.0, shape, jnp.float32)
    exponent = columns[None, None, :] + jitter[None, None, :] + 0.5 * section_pos[:, None, None]
    return (0.1 * jnp.power(10.0, exponent) * base).astype(jnp.bfloat16)


def draw_pre_act(key, part):
    key = jax.random.fold_in(key, 23)
    key_base, key_jitter = jax.random.split(key, 2)
    shape = (SECTIONS, TOK_SECTION, FFW)
    columns = (jnp.arange(FFW, dtype=jnp.float32) + 0.5) / FFW
    jitter = jax.random.uniform(key_jitter, (FFW,), jnp.float32, 0.0, 0.3)
    base = jax.random.truncated_normal(key_base, -6.0, 6.0, shape, jnp.float32)
    exponent = columns[None, None, :] + jitter[None, None, :]
    return (0.3 * jnp.power(10.0, exponent) * base).astype(jnp.bfloat16)


def levels(rng, extent, pieces, least, largest):
    def one(dim, shards_of):
        heights = jax.random.uniform(jax.random.fold_in(jax.random.fold_in(rng, 6), dim), (shards_of,), jnp.float32, least / len(pieces), largest / len(pieces))
        return jnp.repeat(jnp.exp(heights), extent[dim] // shards_of).reshape((-1,) + (1,) * (len(extent) - dim - 1))

    level = one(*pieces[0])
    for cut in pieces[1:]:
        level = level * one(*cut)
    return level


def gaussian(key, shape, scale, most, cuts=(), kind=jnp.bfloat16):
    result = jax.random.normal(key, shape, jnp.float32) * scale
    if len(cuts) > 0:
        result = levels(key, shape, cuts, -0.22, 0.18) * result
    return jnp.clip(result, min=-most, max=most).astype(kind)


def setup_inputs(seed: int = 0) -> dict:
    arg_keys = jax.random.split(jax.random.key(seed), 4)
    grad_out = draw_grad_out(jax.random.fold_in(arg_keys[3], 71), 0)
    pre_act = draw_pre_act(jax.random.fold_in(arg_keys[3], 71), 0)
    w_down = gaussian(arg_keys[2], (SECTIONS, FFW, D), FFW ** -0.5, 0.0390625, ((0, 4), (1, 8), (2, 16)))
    return dict(grad_out=grad_out, pre_act=pre_act, w_down=w_down)


gelu_coef = 0.7978845608028654
cubic_coef = 0.044715
target_rms = 0.5
tiny_eps = 1e-06

def gelu_parts(field):
    tanh_val = jnp.tanh(gelu_coef * (field + cubic_coef * field * field * field))
    values = 0.5 * field * (1.0 + tanh_val)
    slopes = 0.5 * (1.0 + tanh_val) + 0.5 * field * (1.0 - tanh_val * tanh_val) * gelu_coef * (1.0 + 3.0 * cubic_coef * field * field)
    return (values, slopes)

def input_grads(grad_section, pre_section, weight_section):
    act_grad = lax.dot_general(grad_section, weight_section, (((1,), (1,)), ((), ())), preferred_element_type=jnp.float32)
    values, slopes = gelu_parts(pre_section.astype(jnp.float32))
    return ((act_grad * slopes).astype(jnp.bfloat16), values.astype(jnp.bfloat16))

def weight_grad_of(acts, grad_section):
    return lax.dot_general(acts, grad_section, (((0,), (0,)), ((), ())), preferred_element_type=jnp.float32)

def reference(grad_out, pre_act, w_down):

    def first_pass(section_args):
        grad_section, pre_section, weight_section = section_args
        grad_pre, acts = input_grads(grad_section, pre_section, weight_section)
        weight_grad = weight_grad_of(acts, grad_section)
        return (grad_pre, jnp.sum(weight_grad * weight_grad))
    grad_pre, squares = lax.map(first_pass, (grad_out, pre_act, w_down))
    sum_squares = jnp.sum(squares)
    norm_target = target_rms * math.sqrt(float(SECTIONS * FFW * D))
    factor = norm_target / jnp.sqrt(sum_squares + tiny_eps)

    def second_pass(section_args):
        grad_section, pre_section = section_args
        values, slopes = gelu_parts(pre_section.astype(jnp.float32))
        return (weight_grad_of(values.astype(jnp.bfloat16), grad_section) * factor).astype(jnp.bfloat16)
    grad_weight = lax.map(second_pass, (grad_out, pre_act))
    return (grad_pre, grad_weight)
```

```python
import functools
import math

import jax
import jax.numpy as jnp
from jax import lax
from jax.experimental import pallas as pl
from jax.experimental.pallas import tpu as pltpu
from jax.sharding import PartitionSpec as P

MESH = pl.DeviceIdType.MESH

gelu_coef = 0.7978845608028654
cubic_coef = 0.044715
target_rms = 0.5
tiny_eps = 1e-06

ROWS = 16
QUARTERS = 4
PARTS = 2
LAG = 4


def gelu_parts(field):
    tanh_val = jnp.tanh(gelu_coef * (field + cubic_coef * field * field * field))
    values = 0.5 * field * (1.0 + tanh_val)
    slopes = 0.5 * (1.0 + tanh_val) + 0.5 * field * (1.0 - tanh_val * tanh_val) * gelu_coef * (
        1.0 + 3.0 * cubic_coef * field * field
    )
    return (values, slopes)


def encode(v):
    return (v * jnp.abs(v) * (v * v)).astype(jnp.bfloat16)


def decode(code):
    y = code.astype(jnp.float32)
    size = jnp.abs(y)
    root = jnp.sqrt(jnp.sqrt(size))
    return jnp.where(y < 0.0, -root, root)


def kernel(
    n_row, n_col, n_sec, norm_target,
    g_ref, pre_ref, w_hbm, gp_ref, gw_hbm,
    w_buf, acts, packed, slopes_buf, gbuf, gmain, gtail, part, raw, out_buf,
    rs_out, rs_in, peak, ss_row, ss_col, ss_sec,
    w_sem, out_sem, ag_send, ag_recv, rs_send, rs_recv, g_send, g_recv,
    peak_send, peak_recv, ssr_send, ssr_recv, ssc_send, ssc_recv, sss_send, sss_recv,
):
    f32, bf16 = jnp.float32, jnp.bfloat16
    row, col, sec = lax.axis_index("row"), lax.axis_index("col"), lax.axis_index("section")
    hidden, feats = w_buf.shape
    quarter = hidden // QUARTERS
    width = hidden + quarter
    pw = width // PARTS
    extra = pre_ref.shape[1] - ROWS
    half = n_row // 2

    def peer(axis, index, size, d):
        return {axis: lax.rem(index + d, size)}

    row_peers = [peer("row", row, n_row, d) for d in range(n_row)]
    col_peers = [peer("col", col, n_col, d) for d in range(n_col)]
    sec_peers = [peer("section", sec, n_sec, d) for d in range(n_sec)]

    barrier = pltpu.get_barrier_semaphore()
    others = row_peers[1:] + col_peers[1:] + sec_peers[1:]
    for device in others:
        pl.semaphore_signal(barrier, inc=1, device_id=device, device_id_type=MESH)
    w_copy = pltpu.make_async_copy(w_hbm.at[0], w_buf, w_sem)
    w_copy.start()

    pre = pre_ref[0].astype(f32)
    packed[:, pl.ds(0, hidden)] = pre[:ROWS]
    for q in range(QUARTERS):
        packed[pl.ds(q * extra, extra), pl.ds(hidden, quarter)] = pre[ROWS:, q * quarter:(q + 1) * quarter]
    values, slopes = gelu_parts(packed[...])
    acts[0] = values.astype(bf16)
    slopes_buf[...] = slopes

    g = g_ref[0].astype(f32)
    for b in range(2):
        base = b * (ROWS + extra)
        gbuf[0, 0, b] = g[base:base + ROWS].astype(bf16)
        last = g[base + ROWS:base + ROWS + extra]
        gbuf[0, 1, b] = jnp.concatenate([last] * QUARTERS, axis=0).astype(bf16)

    pl.semaphore_wait(barrier, len(others))

    def hops(way, p):
        return half if (way + p) % 2 == 0 else half - 1

    def lanes(p):
        return pl.ds(p * pw, pw)

    def toward(way):
        return row_peers[1] if way == 0 else row_peers[n_row - 1]

    def ag_copy(way, p, h):
        src = (h - 1) if way == 0 else (n_row - h + 1) % n_row
        dst = h if way == 0 else n_row - h
        return pltpu.make_async_remote_copy(
            src_ref=acts.at[src, :, lanes(p)],
            dst_ref=acts.at[dst, :, lanes(p)],
            send_sem=ag_send.at[way, p, h - 1],
            recv_sem=ag_recv.at[way, p, h - 1],
            device_id=toward(way),
            device_id_type=MESH,
        )

    def rs_copy(way, p, k):
        return pltpu.make_async_remote_copy(
            src_ref=rs_out.at[way, p, k - 1],
            dst_ref=rs_in.at[way, p, k - 1],
            send_sem=rs_send.at[way, p, k - 1],
            recv_sem=rs_recv.at[way, p, k - 1],
            device_id=toward(way),
            device_id_type=MESH,
        )

    def spread(buf, send, recv, peers):
        return [
            pltpu.make_async_remote_copy(
                src_ref=buf.at[0], dst_ref=buf.at[d], send_sem=send.at[d], recv_sem=recv.at[d],
                device_id=peers[d], device_id_type=MESH,
            )
            for d in range(1, len(peers))
        ]

    flows = [(way, p) for p in range(PARTS) for way in range(2)]

    def ag_step(h):
        for way, p in flows:
            if h >= 2 and h - 1 <= hops(way, p):
                ag_copy(way, p, h - 1).wait_recv()
            if h <= hops(way, p):
                ag_copy(way, p, h).start()

    ag_step(1)
    g_copies = spread(gbuf, g_send, g_recv, col_peers)
    for c in g_copies:
        c.start()
    ag_step(2)
    w_copy.wait()
    w_peak = jnp.max(jnp.abs(w_buf[...]).astype(f32))
    for c in g_copies:
        c.wait_recv()
    g_peak = jnp.max(jnp.abs(gbuf[...]).astype(f32))
    peak[0] = jnp.full(peak.shape[1:], 1.0, f32) * jnp.maximum(w_peak * g_peak, 1e-30)
    peak_copies = spread(peak, peak_send, peak_recv, row_peers)
    for c in peak_copies:
        c.start()
    ag_step(3)

    for r in range(n_row):
        block = lax.rem(row + (n_row - r), n_row)
        slot = lax.rem(col + n_col - block // 2, n_col)
        which = lax.rem(block, 2)
        gmain[r] = gbuf[slot, 0, which]
        gtail[r] = gbuf[slot, 1, which]

    g_main = gmain[...].reshape(n_row * ROWS, feats)
    g_tail = gtail[...].reshape(n_row * ROWS, feats)
    owner = lax.rem(lax.broadcasted_iota(jnp.int32, g_tail.shape, 0), ROWS) // extra
    g_quarter = [jnp.where(owner == q, g_tail, jnp.zeros_like(g_tail)) for q in range(QUARTERS)]
    tile = 256
    over_feats = (((1,), (1,)), ((), ()))

    def main_tile(t, _):
        at = pl.ds(pl.multiple_of(t * tile, tile), tile)
        res = lax.dot_general(g_main, w_buf[at, :], over_feats, preferred_element_type=f32)
        part[:, :, at] = res.reshape(n_row, ROWS, tile)
        return 0

    lax.fori_loop(0, hidden // tile, main_tile, 0)
    for t in range(quarter // tile):
        res = None
        for q in range(QUARTERS):
            term = lax.dot_general(
                g_quarter[q], w_buf[pl.ds(q * quarter + t * tile, tile), :], over_feats,
                preferred_element_type=f32,
            )
            res = term if res is None else res + term
        part[:, :, pl.ds(hidden + t * tile, tile)] = res.reshape(n_row, ROWS, tile)

    ag_step(4)
    for c in peak_copies:
        c.wait_recv()
    top = jnp.max(peak[...])
    reach = float(n_row * feats)
    scale = (2.0 ** 30 / reach) / top
    unscale = top * (reach / 2.0 ** 30)

    def rs_step(s):
        for way, p in flows:
            k = s - (half - hops(way, p))
            if 1 <= k <= hops(way, p):
                d = hops(way, p) - k + 1
                r = (n_row - d) if way == 0 else d
                v = part[r, :, lanes(p)] * scale
                if k >= 2:
                    rs_copy(way, p, k - 1).wait_recv()
                    v = v + decode(rs_in[way, p, k - 2])
                rs_out[way, p, k - 1] = encode(v)
                rs_copy(way, p, k).start()

    for h in range(5, half + 2):
        ag_step(h)
        rs_step(h - LAG)

    total = None
    over_tokens = (((0,), (0,)), ((), ()))
    a_tail = acts[:, :, pl.ds(hidden, quarter)].reshape(n_row * ROWS, quarter)
    tile_q = quarter // 3
    square = jnp.zeros((8, 128), f32)
    for q in range(QUARTERS):
        for t in range(3):
            at = q * quarter + t * tile_q
            a = acts[:, :, pl.ds(at, tile_q)].reshape(n_row * ROWS, tile_q)
            res = lax.dot_general(a, g_main, over_tokens, preferred_element_type=f32)
            res = res + lax.dot_general(
                a_tail[:, t * tile_q:(t + 1) * tile_q], g_quarter[q], over_tokens,
                preferred_element_type=f32,
            )
            raw[pl.ds(at, tile_q), :] = res
            sq = jnp.sum((res * res).reshape(tile_q // 8, 8, feats), axis=0)
            square = square + (sq[:, :128] + sq[:, 128:256] + sq[:, 256:384])
    ss_row[0] = square
    row_copies = spread(ss_row, ssr_send, ssr_recv, row_peers)
    for c in row_copies:
        c.start()
    first = half + 2 - LAG
    rs_step(first)
    for c in row_copies:
        c.wait_recv()
    ss_col[0] = jnp.sum(ss_row[...], axis=0)
    col_copies = spread(ss_col, ssc_send, ssc_recv, col_peers)
    for c in col_copies:
        c.start()
    rs_step(first + 1)
    for c in col_copies:
        c.wait_recv()
    ss_sec[0] = jnp.sum(ss_col[...], axis=0)
    sec_copies = spread(ss_sec, sss_send, sss_recv, sec_peers)
    for c in sec_copies:
        c.start()
    for s in range(first + 2, half):
        rs_step(s)
    for c in sec_copies:
        c.wait_recv()
    rs_step(half)
    sum_squares = jnp.sum(jnp.sum(ss_sec[...], axis=0), keepdims=True)
    factor = norm_target / jnp.sqrt(sum_squares + tiny_eps)

    out_copies = []
    n_out = 4
    size = hidden // n_out
    for t in range(n_out):
        at = pl.ds(t * size, size)
        out_buf[at, :] = (raw[at, :] * factor).astype(bf16)
        c = pltpu.make_async_copy(out_buf.at[at, :], gw_hbm.at[0, at, :], out_sem.at[t])
        c.start()
        out_copies.append(c)

    for p in range(PARTS):
        arrived = None
        for way in range(2):
            h = hops(way, p)
            rs_copy(way, p, h).wait_recv()
            v = decode(rs_in[way, p, h - 1])
            arrived = v if arrived is None else arrived + v
        act_grad = part[0, :, lanes(p)] + arrived * unscale
        packed[:, lanes(p)] = act_grad * slopes_buf[:, lanes(p)]
    gp_ref[0, pl.ds(0, ROWS), :] = packed[:, pl.ds(0, hidden)].astype(bf16)
    for q in range(QUARTERS):
        gp_ref[0, pl.ds(ROWS, extra), pl.ds(q * quarter, quarter)] = packed[
            pl.ds(q * extra, extra), pl.ds(hidden, quarter)
        ].astype(bf16)

    for way, p in flows:
        for h in range(1, hops(way, p) + 1):
            ag_copy(way, p, h).wait_send()
            rs_copy(way, p, h).wait_send()
    for copies in (g_copies, peak_copies, row_copies, col_copies, sec_copies):
        for c in copies:
            c.wait_send()
    for c in out_copies:
        c.wait()


def on_device(sizes, grad_out, pre_act, w_down):
    n_sec, n_row, n_col = sizes
    f32, bf16 = jnp.float32, jnp.bfloat16
    _, hidden, feats = w_down.shape
    quarter = hidden // QUARTERS
    width = hidden + quarter
    half = n_row // 2
    norm_target = target_rms * math.sqrt(float(n_sec * hidden * n_col * feats * n_row))
    dma = pltpu.SemaphoreType.DMA
    ring = (2, PARTS, half)
    vmem = pl.BlockSpec(memory_space=pltpu.VMEM)
    hbm = pl.BlockSpec(memory_space=pl.ANY)
    return pl.pallas_call(
        functools.partial(kernel, n_row, n_col, n_sec, norm_target),
        out_shape=(
            jax.ShapeDtypeStruct(pre_act.shape, bf16),
            jax.ShapeDtypeStruct(w_down.shape, bf16),
        ),
        in_specs=[vmem, vmem, hbm],
        out_specs=(vmem, hbm),
        scratch_shapes=[
            pltpu.VMEM((hidden, feats), bf16),
            pltpu.VMEM((n_row, ROWS, width), bf16),
            pltpu.VMEM((ROWS, width), f32),
            pltpu.VMEM((ROWS, width), f32),
            pltpu.VMEM((n_col, 2, 2, ROWS, feats), bf16),
            pltpu.VMEM((n_row, ROWS, feats), bf16),
            pltpu.VMEM((n_row, ROWS, feats), bf16),
            pltpu.VMEM((n_row, ROWS, width), f32),
            pltpu.VMEM((hidden, feats), f32),
            pltpu.VMEM((hidden, feats), bf16),
            pltpu.VMEM(ring + (ROWS, width // PARTS), bf16),
            pltpu.VMEM(ring + (ROWS, width // PARTS), bf16),
            pltpu.VMEM((n_row, 8, 128), f32),
            pltpu.VMEM((n_row, 8, 128), f32),
            pltpu.VMEM((n_col, 8, 128), f32),
            pltpu.VMEM((n_sec, 8, 128), f32),
            dma, dma((4,)),
            dma(ring), dma(ring), dma(ring), dma(ring),
            dma((n_col,)), dma((n_col,)),
            dma((n_row,)), dma((n_row,)),
            dma((n_row,)), dma((n_row,)),
            dma((n_col,)), dma((n_col,)),
            dma((n_sec,)), dma((n_sec,)),
        ],
        compiler_params=pltpu.CompilerParams(
            collective_id=0, has_side_effects=True, vmem_limit_bytes=56 * 1024 * 1024
        ),
        cost_estimate=pl.CostEstimate(
            flops=4 * 320 * hidden * feats, bytes_accessed=4 * hidden * feats, transcendentals=0
        ),
    )(grad_out, pre_act, w_down)


def solution(mesh):
    sizes = (mesh.shape["section"], mesh.shape["row"], mesh.shape["col"])
    in_specs = (P("section", "col", "row"), P("section", "row", "col"), P("section", "col", "row"))
    out_specs = (P("section", "row", "col"), P("section", "col", "row"))
    return jax.shard_map(
        functools.partial(on_device, sizes), mesh=mesh, in_specs=in_specs, out_specs=out_specs,
        check_vma=False,
    )
```

```python
import functools
import math

import jax
import jax.numpy as jnp
from jax import lax
from jax.experimental import pallas as pl
from jax.experimental.pallas import tpu as pltpu
from jax.sharding import PartitionSpec as P

MESH = pl.DeviceIdType.MESH

gelu_coef = 0.7978845608028654
cubic_coef = 0.044715
target_rms = 0.5
tiny_eps = 1e-06

ROWS = 16
QUARTERS = 4
AG_PARTS = 3
RS_PARTS = 3
ORDER = (
    "ag1", "send_g", "ag2", "bound_w", "ag3", "wait_g", "order_g",
    "bound_g", "sums_main", "ag4", "sums_tail", "rs1", "ag5", "ag6",
    "rs2", "ag7", "rs3", "ag8", "rs4", "ag9", "weight_grad",
    "send_squares", "rs5", "rs6", "row_sums", "rs7", "col_sums", "rs8",
    "finish_factor", "grad_pre",
)


def gelu_parts(field):
    tanh_val = jnp.tanh(gelu_coef * (field + cubic_coef * field * field * field))
    values = 0.5 * field * (1.0 + tanh_val)
    slopes = 0.5 * (1.0 + tanh_val) + 0.5 * field * (1.0 - tanh_val * tanh_val) * gelu_coef * (
        1.0 + 3.0 * cubic_coef * field * field
    )
    return (values, slopes)


def encode(v):
    return (v * jnp.abs(v) * (v * v)).astype(jnp.bfloat16)


def decode(code):
    y = code.astype(jnp.float32)
    inverse = lax.rsqrt(jnp.maximum(jnp.abs(y), 2.0 ** -120))
    return (y * inverse) * (inverse * lax.rsqrt(inverse))


def kernel(
    n_row, n_col, n_sec, norm_target,
    g_hbm, pre_hbm, w_hbm, gp_ref, raw, factor_ref,
    g_ref, pre_ref,
    w_buf, acts, packed, slopes_buf, gbuf, gmain, gtail, part,
    lead_out, lead_in, rs_out, rs_in, bounds, ss_row, ss_col, ss_sec,
    in_sem, w_sem, ag_send, ag_recv, lead_send, lead_recv, rs_send, rs_recv, g_sem, sr_sem, sc_sem, ss_sem,
):
    f32, bf16 = jnp.float32, jnp.bfloat16
    row, col, sec = lax.axis_index("row"), lax.axis_index("col"), lax.axis_index("section")
    hidden, feats = w_buf.shape
    quarter = hidden // QUARTERS
    width = hidden + quarter
    extra = pre_ref.shape[1] - ROWS
    half = n_row // 2

    def peer(axis, index, size, d):
        return {axis: lax.rem(index + d, size)}

    row_peers = [peer("row", row, n_row, d) for d in range(n_row)]
    col_peers = [peer("col", col, n_col, d) for d in range(n_col)]
    sec_peers = [peer("section", sec, n_sec, d) for d in range(n_sec)]

    barrier = pltpu.get_barrier_semaphore()
    others = [row_peers[1], row_peers[n_row - 1]] + col_peers[1:] + sec_peers[1:]
    for device in others:
        pl.semaphore_signal(barrier, inc=1, device_id=device, device_id_type=MESH)
    w_copy = pltpu.make_async_copy(w_hbm.at[0], w_buf, w_sem)
    in_copies = [
        pltpu.make_async_copy(pre_hbm, pre_ref, in_sem.at[0]),
        pltpu.make_async_copy(g_hbm, g_ref, in_sem.at[1]),
    ]
    for c in in_copies:
        c.start()
    w_copy.start()
    for c in in_copies:
        c.wait()

    pre = pre_ref[0].astype(f32)
    packed[:, pl.ds(0, hidden)] = pre[:ROWS]
    for q in range(QUARTERS):
        packed[pl.ds(q * extra, extra), pl.ds(hidden, quarter)] = pre[ROWS:, q * quarter:(q + 1) * quarter]
    values, slopes = gelu_parts(packed[...])
    acts[0] = values.astype(bf16)
    slopes_buf[...] = slopes

    g = g_ref[0].astype(f32)
    for b in range(2):
        base = b * (ROWS + extra)
        gbuf[0, 0, b] = g[base:base + ROWS].astype(bf16)
        last = g[base + ROWS:base + ROWS + extra]
        gbuf[0, 1, b] = jnp.concatenate([last] * QUARTERS, axis=0).astype(bf16)

    pl.semaphore_wait(barrier, len(others))

    def flows(parts):
        return [(way, p) for p in range(parts) for way in range(2)]

    def hops(way, p):
        return half if (way + p) % 2 == 0 else half - 1

    def lanes(p, parts):
        return pl.ds(p * (width // parts), width // parts)

    def places(parts, lead):
        keys = [
            (way, p, j) for way, p in flows(parts) for j in range(1, hops(way, p) + 1)
            if not (lead and p == way)
        ]
        return {key: i for i, key in enumerate(keys)}

    ag_place, rs_place = places(AG_PARTS, False), places(RS_PARTS, True)

    def onward(way):
        return row_peers[1 if way == 0 else n_row - 1]

    def ag_copy(way, p, j):
        src, dst = (j - 1, j) if way == 0 else ((n_row - j + 1) % n_row, n_row - j)
        at = lanes(p, AG_PARTS)
        return pltpu.make_async_remote_copy(
            src_ref=acts.at[src, :, at], dst_ref=acts.at[dst, :, at],
            send_sem=ag_send, recv_sem=ag_recv.at[ag_place[way, p, j]],
            device_id=onward(way), device_id_type=MESH,
        )

    def rs_slot(way, p, j, out):
        if p == way:
            return (lead_out if out else lead_in).at[way * half + j - 1]
        return (rs_out if out else rs_in).at[rs_place[way, p, j]]

    def rs_copy(way, p, j):
        lead = p == way
        return pltpu.make_async_remote_copy(
            src_ref=rs_slot(way, p, j, True), dst_ref=rs_slot(way, p, j, False),
            send_sem=lead_send if lead else rs_send,
            recv_sem=lead_recv.at[way * half + j - 1] if lead else rs_recv.at[rs_place[way, p, j]],
            device_id=onward(way), device_id_type=MESH,
        )

    def spread(buf, sems, peers):
        for d in range(1, len(peers)):
            pltpu.make_async_remote_copy(
                src_ref=buf.at[0], dst_ref=buf.at[d], send_sem=sems.at[0], recv_sem=sems.at[1],
                device_id=peers[d], device_id_type=MESH,
            ).start()

    def whole(buf, send_sem, recv_sem, count):
        every = buf.at[pl.ds(buf.shape[0] - count, count)]
        return pltpu.make_async_remote_copy(
            src_ref=every, dst_ref=every, send_sem=send_sem, recv_sem=recv_sem,
            device_id=row_peers[1], device_id_type=MESH,
        )

    def gathered(buf, sems):
        whole(buf, sems.at[0], sems.at[1], buf.shape[0] - 1).wait_recv()

    def ag_part(h, way, p):
        if 1 <= h - 1 <= hops(way, p):
            ag_copy(way, p, h - 1).wait_recv()
        if h <= hops(way, p):
            ag_copy(way, p, h).start()

    def ag_step(h):
        for way, p in flows(AG_PARTS):
            ag_part(h, way, p)

    over_feats = (((1,), (1,)), ((), ()))
    over_tokens = (((0,), (0,)), ((), ()))
    def order_g():
        for r in range(n_row):
            block = lax.rem(row + (n_row - r), n_row)
            slot = lax.rem(col + n_col - block // 2, n_col)
            which = lax.rem(block, 2)
            gmain[r] = gbuf[slot, 0, which]
            gtail[r] = gbuf[slot, 1, which]

    def g_blocks():
        g_main = gmain[...].reshape(n_row * ROWS, feats)
        g_tail = gtail[...].reshape(n_row * ROWS, feats)
        owner = lax.rem(lax.broadcasted_iota(jnp.int32, g_tail.shape, 0), ROWS) // extra
        return g_main, [jnp.where(owner == q, g_tail, jnp.zeros_like(g_tail)) for q in range(QUARTERS)]

    tile = 256

    def sums_main():
        g_main, _ = g_blocks()

        def main_tile(t, _):
            at = pl.ds(pl.multiple_of(t * tile, tile), tile)
            res = lax.dot_general(g_main, w_buf[at, :], over_feats, preferred_element_type=f32)
            part[:, :, at] = res.reshape(n_row, ROWS, tile)
            return 0

        lax.fori_loop(0, hidden // tile, main_tile, 0)

    def sums_tail():
        _, g_quarter = g_blocks()
        for t in range(quarter // tile):
            res = None
            for q in range(QUARTERS):
                term = lax.dot_general(
                    g_quarter[q], w_buf[pl.ds(q * quarter + t * tile, tile), :], over_feats,
                    preferred_element_type=f32,
                )
                res = term if res is None else res + term
            part[:, :, pl.ds(hidden + t * tile, tile)] = res.reshape(n_row, ROWS, tile)

    def bound_w():
        w_copy.wait()
        bounds[0] = jnp.full(bounds.shape[1:], jnp.max(jnp.abs(w_buf[...]).astype(f32)))

    def bound_g():
        top = bounds[0] * (jnp.max(jnp.abs(gbuf[...]).astype(f32)) * feats)
        bounds[0] = jnp.maximum(top, 1e-30)

    one = 2.0 ** 27
    pw = width // RS_PARTS

    def wide(block):
        return jnp.concatenate([block] * (pw // 128), axis=1)

    def received(way, p, j):
        return decode(rs_slot(way, p, j, False)[:, pl.ds(0, pw)])

    def bound_in(way, j):
        return rs_slot(way, way, j, False)[:, pl.ds(pw, 128)].astype(f32)

    def parts_of(way):
        return [way] + [p for p in range(RS_PARTS) if p != way]

    scales = {}

    def rs_part(s, way, p):
        j = half + 1 - s
        if j > hops(way, p):
            return
        if j < hops(way, p):
            rs_copy(way, p, j + 1).wait_recv()
        if p == way:
            bound = bounds[0]
            back = None
            if j < half:
                into = bound_in(way, j + 1)
                bound = jnp.maximum(bound, into)
                back = wide(into * (1.0 / one))
            bound = bound.astype(bf16)
            rs_slot(way, p, j, True)[:, pl.ds(pw, 128)] = bound
            scales[way] = wide(one / bound.astype(f32)), back
        scale, back = scales[way]
        v = part[(n_row - j) if way == 0 else j, :, lanes(p, RS_PARTS)]
        if j < hops(way, p):
            v = v + received(way, p, j + 1) * back
        rs_slot(way, p, j, True)[:, pl.ds(0, pw)] = encode(v * scale)
        rs_copy(way, p, j).start()

    def rs_step(s):
        for i in range(RS_PARTS):
            for way in range(2):
                rs_part(s, way, parts_of(way)[i])

    def weight_grad():
        g_main, g_quarter = g_blocks()
        a_tail = acts[:, :, pl.ds(hidden, quarter)].reshape(n_row * ROWS, quarter)
        size = quarter // 3
        square = jnp.zeros((8, 128), f32)
        for q in range(QUARTERS):
            for t in range(3):
                at = q * quarter + t * size
                a = acts[:, :, pl.ds(at, size)].reshape(n_row * ROWS, size)
                res = lax.dot_general(a, g_main, over_tokens, preferred_element_type=f32)
                res = res + lax.dot_general(
                    a_tail[:, t * size:(t + 1) * size], g_quarter[q], over_tokens,
                    preferred_element_type=f32,
                )
                raw[pl.ds(at, size), :] = res
                sq = jnp.sum((res * res).reshape(size // 8, 8, feats), axis=0)
                for c in range(feats // 128):
                    square = square + sq[:, c * 128:(c + 1) * 128]
        ss_row[0] = square

    def finish_factor():
        gathered(ss_sec, ss_sem)
        sum_squares = jnp.sum(jnp.sum(ss_sec[...], axis=0), keepdims=True)
        factor_ref[...] = jnp.broadcast_to(norm_target / jnp.sqrt(sum_squares + tiny_eps), (8, 128))

    def grad_pre():
        back = []
        for way in range(2):
            rs_copy(way, way, 1).wait_recv()
            back.append(wide(bound_in(way, 1) * (1.0 / one)))
        for p in range(RS_PARTS):
            at = lanes(p, RS_PARTS)
            act_grad = part[0, :, at]
            for way in range(2):
                if p != way:
                    rs_copy(way, p, 1).wait_recv()
                act_grad = act_grad + received(way, p, 1) * back[way]
            packed[:, at] = act_grad * slopes_buf[:, at]
        gp_ref[0, pl.ds(0, ROWS), :] = packed[:, pl.ds(0, hidden)].astype(bf16)
        for q in range(QUARTERS):
            gp_ref[0, pl.ds(ROWS, extra), pl.ds(q * quarter, quarter)] = packed[
                pl.ds(q * extra, extra), pl.ds(hidden, quarter)
            ].astype(bf16)

    def row_sums():
        gathered(ss_row, sr_sem)
        ss_col[0] = jnp.sum(ss_row[...], axis=0)
        spread(ss_col, sc_sem, col_peers)

    def col_sums():
        gathered(ss_col, sc_sem)
        ss_sec[0] = jnp.sum(ss_col[...], axis=0)
        spread(ss_sec, ss_sem, sec_peers)

    steps = dict(
        bound_w=bound_w,
        bound_g=bound_g,
        send_g=lambda: spread(gbuf, g_sem, col_peers),
        wait_g=lambda: gathered(gbuf, g_sem),
        order_g=order_g,
        sums_main=sums_main,
        sums_tail=sums_tail,
        weight_grad=weight_grad,
        send_squares=lambda: spread(ss_row, sr_sem, row_peers),
        row_sums=row_sums,
        col_sums=col_sums,
        finish_factor=finish_factor,
        grad_pre=grad_pre,
    )
    for h in range(1, half + 2):
        steps["ag%d" % h] = functools.partial(ag_step, h)
        steps["rs%d" % h] = functools.partial(rs_step, h)
    for name in ORDER:
        steps[name]()

    whole(acts, ag_send, ag_recv.at[0], n_row - 1).wait_send()
    whole(lead_out, lead_send, lead_recv.at[0], lead_out.shape[0]).wait_send()
    whole(rs_out, rs_send, rs_recv.at[0], rs_out.shape[0]).wait_send()
    for buf, sems in (
        (gbuf, g_sem), (ss_row, sr_sem), (ss_col, sc_sem), (ss_sec, ss_sem),
    ):
        whole(buf, sems.at[0], sems.at[1], buf.shape[0] - 1).wait_send()


def scale_kernel(n_out, raw, factor_ref, gp_ref, gw_hbm, gp_hbm, out_buf, sems):
    gp_copy = pltpu.make_async_copy(gp_ref, gp_hbm, sems.at[n_out])
    gp_copy.start()
    factor = factor_ref[0:1, 0:1]
    size = raw.shape[0] // n_out
    copies = []
    for t in range(n_out):
        at = pl.ds(t * size, size)
        out_buf[at, :] = (raw[at, :] * factor).astype(jnp.bfloat16)
        c = pltpu.make_async_copy(out_buf.at[at, :], gw_hbm.at[0, at, :], sems.at[t])
        c.start()
        copies.append(c)
    for c in copies:
        c.wait()
    gp_copy.wait()


def on_device(sizes, grad_out, pre_act, w_down):
    n_sec, n_row, n_col = sizes
    f32, bf16 = jnp.float32, jnp.bfloat16
    _, hidden, feats = w_down.shape
    width = hidden + hidden // QUARTERS
    norm_target = target_rms * math.sqrt(float(n_sec * hidden * n_col * feats * n_row))
    dma = pltpu.SemaphoreType.DMA
    n_ag, n_rs = AG_PARTS * (n_row - 1), RS_PARTS * (n_row - 1) - n_row
    vmem = pl.BlockSpec(memory_space=pltpu.VMEM)
    hbm = pl.BlockSpec(memory_space=pl.ANY)
    small = (8, 128)
    gp, raw, factor = pl.pallas_call(
        functools.partial(kernel, n_row, n_col, n_sec, norm_target),
        out_shape=(
            pltpu.VMEM(pre_act.shape, bf16),
            pltpu.VMEM((hidden, feats), f32),
            pltpu.VMEM(small, f32),
        ),
        in_specs=[hbm, hbm, hbm],
        out_specs=(vmem, vmem, vmem),
        scratch_shapes=[
            pltpu.VMEM(grad_out.shape, bf16),
            pltpu.VMEM(pre_act.shape, bf16),
            pltpu.VMEM((hidden, feats), bf16),
            pltpu.VMEM((n_row, ROWS, width), bf16),
            pltpu.VMEM((ROWS, width), f32),
            pltpu.VMEM((ROWS, width), f32),
            pltpu.VMEM((n_col, 2, 2, ROWS, feats), bf16),
            pltpu.VMEM((n_row, ROWS, feats), bf16),
            pltpu.VMEM((n_row, ROWS, feats), bf16),
            pltpu.VMEM((n_row, ROWS, width), f32),
            pltpu.VMEM((n_row, ROWS, width // RS_PARTS + 128), bf16),
            pltpu.VMEM((n_row, ROWS, width // RS_PARTS + 128), bf16),
            pltpu.VMEM((n_rs, ROWS, width // RS_PARTS), bf16),
            pltpu.VMEM((n_rs, ROWS, width // RS_PARTS), bf16),
            pltpu.VMEM((1, ROWS, 128), f32),
            pltpu.VMEM((n_row,) + small, f32),
            pltpu.VMEM((n_col,) + small, f32),
            pltpu.VMEM((n_sec,) + small, f32),
            dma((2,)), dma, dma, dma((n_ag,)), dma, dma((n_row,)), dma, dma((n_rs,)),
            dma((2,)), dma((2,)), dma((2,)), dma((2,)),
        ],
        compiler_params=pltpu.CompilerParams(
            collective_id=0, has_side_effects=True, vmem_limit_bytes=58 * 1024 * 1024
        ),
        cost_estimate=pl.CostEstimate(
            flops=4 * 320 * hidden * feats, bytes_accessed=4 * hidden * feats, transcendentals=0
        ),
    )(grad_out, pre_act, w_down)
    n_out = 4
    gw, gp = pl.pallas_call(
        functools.partial(scale_kernel, n_out),
        out_shape=(
            jax.ShapeDtypeStruct(w_down.shape, bf16),
            jax.ShapeDtypeStruct(pre_act.shape, bf16),
        ),
        in_specs=[vmem, vmem, vmem],
        out_specs=(hbm, hbm),
        scratch_shapes=[pltpu.VMEM((hidden, feats), bf16), dma((n_out + 1,))],
        compiler_params=pltpu.CompilerParams(vmem_limit_bytes=16 * 1024 * 1024),
    )(raw, factor, gp)
    return gp, gw


def solution(mesh):
    sizes = (mesh.shape["section"], mesh.shape["row"], mesh.shape["col"])
    in_specs = (P("section", "col", "row"), P("section", "row", "col"), P("section", "col", "row"))
    out_specs = (P("section", "row", "col"), P("section", "col", "row"))
    return jax.shard_map(
        functools.partial(on_device, sizes), mesh=mesh, in_specs=in_specs, out_specs=out_specs,
        check_vma=False,
    )
```

```python
import functools
import math

import jax
import jax.numpy as jnp
from jax import lax
from jax.experimental import pallas as pl
from jax.experimental.pallas import tpu as pltpu
from jax.sharding import PartitionSpec as P

MESH = pl.DeviceIdType.MESH

gelu_coef = 0.7978845608028654
cubic_coef = 0.044715
target_rms = 0.5
tiny_eps = 1e-06

ROWS = 16
QUARTERS = 4
AG_PARTS = 3
RS_PARTS = 3
ORDER = (
    "ag1", "send_g", "slopes", "ag2", "bound_w", "ag3", "wait_g",
    "order_g", "bound_g", "sums_main", "ag4", "sums_tail", "rs1", "ag5",
    "ag6", "rs2", "ag7", "rs3", "ag8", "rs4", "ag9",
    "weight_grad", "send_squares", "rs5", "rs6", "row_sums", "rs7", "rs8",
    "col_sums", "grad_pre", "finish_factor",
)


def gelu_tanh(field):
    return jnp.tanh(gelu_coef * (field + cubic_coef * field * field * field))


def gelu_values(field):
    return 0.5 * field * (1.0 + gelu_tanh(field))


def gelu_slopes(field):
    tanh_val = gelu_tanh(field)
    return 0.5 * (1.0 + tanh_val) + 0.5 * field * (1.0 - tanh_val * tanh_val) * gelu_coef * (
        1.0 + 3.0 * cubic_coef * field * field
    )


def encode(v):
    return (v * jnp.abs(v) * (v * v)).astype(jnp.bfloat16)


def decode(code):
    y = code.astype(jnp.float32)
    inverse = lax.rsqrt(jnp.maximum(jnp.abs(y), 2.0 ** -120))
    return (y * inverse) * (inverse * lax.rsqrt(inverse))


def kernel(
    n_row, n_col, n_sec, norm_target,
    g_hbm, pre_hbm, w_hbm, gp_ref, raw, factor_ref,
    g_ref, pre_ref,
    w_buf, acts, packed, slopes_buf, gbuf, gmain, gtail, part,
    lead_out, lead_in, rs_out, rs_in, bounds, ss_row, ss_col, ss_sec,
    in_sem, w_sem, ag_send, ag_recv, lead_send, lead_recv, rs_send, rs_recv, g_sem, sr_sem, sc_sem, ss_sem,
):
    f32, bf16 = jnp.float32, jnp.bfloat16
    row, col, sec = lax.axis_index("row"), lax.axis_index("col"), lax.axis_index("section")
    hidden, feats = w_buf.shape
    quarter = hidden // QUARTERS
    width = hidden + quarter
    extra = pre_ref.shape[1] - ROWS
    half = n_row // 2

    def peer(axis, index, size, d):
        return {axis: lax.rem(index + d, size)}

    row_peers = [peer("row", row, n_row, d) for d in range(n_row)]
    col_peers = [peer("col", col, n_col, d) for d in range(n_col)]
    sec_peers = [peer("section", sec, n_sec, d) for d in range(n_sec)]

    barrier = pltpu.get_barrier_semaphore()
    others = [row_peers[1], row_peers[n_row - 1]] + col_peers[1:] + sec_peers[1:]
    for device in others:
        pl.semaphore_signal(barrier, inc=1, device_id=device, device_id_type=MESH)
    w_copy = pltpu.make_async_copy(w_hbm.at[0], w_buf, w_sem)
    in_copies = [
        pltpu.make_async_copy(pre_hbm, pre_ref, in_sem.at[0]),
        pltpu.make_async_copy(g_hbm, g_ref, in_sem.at[1]),
    ]
    for c in in_copies:
        c.start()
    w_copy.start()
    in_copies[0].wait()
    pre = pre_ref[0].astype(f32)
    packed[:, pl.ds(0, hidden)] = pre[:ROWS]
    for q in range(QUARTERS):
        packed[pl.ds(q * extra, extra), pl.ds(hidden, quarter)] = pre[ROWS:, q * quarter:(q + 1) * quarter]
    acts[0] = gelu_values(packed[...]).astype(bf16)

    pl.semaphore_wait(barrier, len(others))

    def flows(parts):
        return [(way, p) for p in range(parts) for way in range(2)]

    def hops(way, p):
        return half if (way + p) % 2 == 0 else half - 1

    def lanes(p, parts):
        return pl.ds(p * (width // parts), width // parts)

    def places(parts, lead):
        keys = [
            (way, p, j) for way, p in flows(parts) for j in range(1, hops(way, p) + 1)
            if not (lead and p == way)
        ]
        return {key: i for i, key in enumerate(keys)}

    ag_place, rs_place = places(AG_PARTS, False), places(RS_PARTS, True)

    def onward(way):
        return row_peers[1 if way == 0 else n_row - 1]

    def ag_copy(way, p, j):
        src, dst = (j - 1, j) if way == 0 else ((n_row - j + 1) % n_row, n_row - j)
        at = lanes(p, AG_PARTS)
        return pltpu.make_async_remote_copy(
            src_ref=acts.at[src, :, at], dst_ref=acts.at[dst, :, at],
            send_sem=ag_send, recv_sem=ag_recv.at[ag_place[way, p, j]],
            device_id=onward(way), device_id_type=MESH,
        )

    def rs_slot(way, p, j, out):
        if p == way:
            return (lead_out if out else lead_in).at[way * half + j - 1]
        return (rs_out if out else rs_in).at[rs_place[way, p, j]]

    def rs_copy(way, p, j):
        lead = p == way
        return pltpu.make_async_remote_copy(
            src_ref=rs_slot(way, p, j, True), dst_ref=rs_slot(way, p, j, False),
            send_sem=lead_send if lead else rs_send,
            recv_sem=lead_recv.at[way * half + j - 1] if lead else rs_recv.at[rs_place[way, p, j]],
            device_id=onward(way), device_id_type=MESH,
        )

    def spread(buf, sems, peers):
        for d in range(1, len(peers)):
            pltpu.make_async_remote_copy(
                src_ref=buf.at[0], dst_ref=buf.at[d], send_sem=sems.at[0], recv_sem=sems.at[1],
                device_id=peers[d], device_id_type=MESH,
            ).start()

    def whole(buf, send_sem, recv_sem, count):
        every = buf.at[pl.ds(buf.shape[0] - count, count)]
        return pltpu.make_async_remote_copy(
            src_ref=every, dst_ref=every, send_sem=send_sem, recv_sem=recv_sem,
            device_id=row_peers[1], device_id_type=MESH,
        )

    def gathered(buf, sems):
        whole(buf, sems.at[0], sems.at[1], buf.shape[0] - 1).wait_recv()

    def ag_part(h, way, p):
        if 1 <= h - 1 <= hops(way, p):
            ag_copy(way, p, h - 1).wait_recv()
        if h <= hops(way, p):
            ag_copy(way, p, h).start()

    def ag_step(h):
        for way, p in flows(AG_PARTS):
            ag_part(h, way, p)

    def pack_g():
        in_copies[1].wait()
        g = g_ref[0].astype(f32)
        for b in range(2):
            base = b * (ROWS + extra)
            gbuf[0, 0, b] = g[base:base + ROWS].astype(bf16)
            last = g[base + ROWS:base + ROWS + extra]
            gbuf[0, 1, b] = jnp.concatenate([last] * QUARTERS, axis=0).astype(bf16)
        spread(gbuf, g_sem, col_peers)

    def slopes():
        slopes_buf[...] = gelu_slopes(packed[...])

    over_feats = (((1,), (1,)), ((), ()))
    over_tokens = (((0,), (0,)), ((), ()))
    def order_g():
        for r in range(n_row):
            block = lax.rem(row + (n_row - r), n_row)
            slot = lax.rem(col + n_col - block // 2, n_col)
            which = lax.rem(block, 2)
            gmain[r] = gbuf[slot, 0, which]
            gtail[r] = gbuf[slot, 1, which]

    def g_blocks():
        g_main = gmain[...].reshape(n_row * ROWS, feats)
        g_tail = gtail[...].reshape(n_row * ROWS, feats)
        owner = lax.rem(lax.broadcasted_iota(jnp.int32, g_tail.shape, 0), ROWS) // extra
        return g_main, [jnp.where(owner == q, g_tail, jnp.zeros_like(g_tail)) for q in range(QUARTERS)]

    tile = 256

    def sums_main():
        g_main, _ = g_blocks()

        def main_tile(t, _):
            at = pl.ds(pl.multiple_of(t * tile, tile), tile)
            res = lax.dot_general(g_main, w_buf[at, :], over_feats, preferred_element_type=f32)
            part[:, :, at] = res.reshape(n_row, ROWS, tile)
            return 0

        lax.fori_loop(0, hidden // tile, main_tile, 0)

    def sums_tail():
        _, g_quarter = g_blocks()
        for t in range(quarter // tile):
            res = None
            for q in range(QUARTERS):
                term = lax.dot_general(
                    g_quarter[q], w_buf[pl.ds(q * quarter + t * tile, tile), :], over_feats,
                    preferred_element_type=f32,
                )
                res = term if res is None else res + term
            part[:, :, pl.ds(hidden + t * tile, tile)] = res.reshape(n_row, ROWS, tile)

    def bound_w():
        w_copy.wait()
        bounds[0] = jnp.full(bounds.shape[1:], jnp.max(jnp.abs(w_buf[...]).astype(f32)))

    def bound_g():
        top = bounds[0] * (jnp.max(jnp.abs(gbuf[...]).astype(f32)) * feats)
        bounds[0] = jnp.maximum(top, 1e-30)

    one = 2.0 ** 27
    pw = width // RS_PARTS

    def wide(block):
        return jnp.concatenate([block] * (pw // 128), axis=1)

    def received(way, p, j):
        return decode(rs_slot(way, p, j, False)[:, pl.ds(0, pw)])

    def bound_in(way, j):
        return rs_slot(way, way, j, False)[:, pl.ds(pw, 128)].astype(f32)

    def parts_of(way):
        return [way] + [p for p in range(RS_PARTS) if p != way]

    scales = {}

    def rs_part(s, way, p):
        j = half + 1 - s
        if j > hops(way, p):
            return
        if j < hops(way, p):
            rs_copy(way, p, j + 1).wait_recv()
        if p == way:
            bound = bounds[0]
            back = None
            if j < half:
                into = bound_in(way, j + 1)
                bound = jnp.maximum(bound, into)
                back = wide(into * (1.0 / one))
            bound = bound.astype(bf16)
            rs_slot(way, p, j, True)[:, pl.ds(pw, 128)] = bound
            scales[way] = wide(one / bound.astype(f32)), back
        scale, back = scales[way]
        v = part[(n_row - j) if way == 0 else j, :, lanes(p, RS_PARTS)]
        if j < hops(way, p):
            v = v + received(way, p, j + 1) * back
        rs_slot(way, p, j, True)[:, pl.ds(0, pw)] = encode(v * scale)
        rs_copy(way, p, j).start()

    def rs_step(s):
        for i in range(RS_PARTS):
            for way in range(2):
                rs_part(s, way, parts_of(way)[i])

    def weight_grad():
        g_main, g_quarter = g_blocks()
        a_tail = acts[:, :, pl.ds(hidden, quarter)].reshape(n_row * ROWS, quarter)
        size = quarter // 3
        square = jnp.zeros((8, 128), f32)
        for q in range(QUARTERS):
            for t in range(3):
                at = q * quarter + t * size
                a = acts[:, :, pl.ds(at, size)].reshape(n_row * ROWS, size)
                res = lax.dot_general(a, g_main, over_tokens, preferred_element_type=f32)
                res = res + lax.dot_general(
                    a_tail[:, t * size:(t + 1) * size], g_quarter[q], over_tokens,
                    preferred_element_type=f32,
                )
                raw[pl.ds(at, size), :] = res
                sq = jnp.sum((res * res).reshape(size // 8, 8, feats), axis=0)
                for c in range(feats // 128):
                    square = square + sq[:, c * 128:(c + 1) * 128]
        ss_row[0] = square

    def finish_factor():
        gathered(ss_sec, ss_sem)
        sum_squares = jnp.sum(jnp.sum(ss_sec[...], axis=0), keepdims=True)
        factor_ref[...] = jnp.broadcast_to(norm_target / jnp.sqrt(sum_squares + tiny_eps), (8, 128))

    def grad_pre():
        back = []
        for way in range(2):
            rs_copy(way, way, 1).wait_recv()
            back.append(wide(bound_in(way, 1) * (1.0 / one)))
        for p in range(RS_PARTS):
            at = lanes(p, RS_PARTS)
            act_grad = part[0, :, at]
            for way in range(2):
                if p != way:
                    rs_copy(way, p, 1).wait_recv()
                act_grad = act_grad + received(way, p, 1) * back[way]
            packed[:, at] = act_grad * slopes_buf[:, at]
        gp_ref[0, pl.ds(0, ROWS), :] = packed[:, pl.ds(0, hidden)].astype(bf16)
        for q in range(QUARTERS):
            gp_ref[0, pl.ds(ROWS, extra), pl.ds(q * quarter, quarter)] = packed[
                pl.ds(q * extra, extra), pl.ds(hidden, quarter)
            ].astype(bf16)

    def row_sums():
        gathered(ss_row, sr_sem)
        ss_col[0] = jnp.sum(ss_row[...], axis=0)
        spread(ss_col, sc_sem, col_peers)

    def col_sums():
        gathered(ss_col, sc_sem)
        ss_sec[0] = jnp.sum(ss_col[...], axis=0)
        spread(ss_sec, ss_sem, sec_peers)

    steps = dict(
        bound_w=bound_w,
        bound_g=bound_g,
        send_g=pack_g,
        slopes=slopes,
        wait_g=lambda: gathered(gbuf, g_sem),
        order_g=order_g,
        sums_main=sums_main,
        sums_tail=sums_tail,
        weight_grad=weight_grad,
        send_squares=lambda: spread(ss_row, sr_sem, row_peers),
        row_sums=row_sums,
        col_sums=col_sums,
        finish_factor=finish_factor,
        grad_pre=grad_pre,
    )
    for h in range(1, half + 2):
        steps["ag%d" % h] = functools.partial(ag_step, h)
        steps["rs%d" % h] = functools.partial(rs_step, h)
    for name in ORDER:
        steps[name]()

    whole(acts, ag_send, ag_recv.at[0], n_row - 1).wait_send()
    whole(lead_out, lead_send, lead_recv.at[0], lead_out.shape[0]).wait_send()
    whole(rs_out, rs_send, rs_recv.at[0], rs_out.shape[0]).wait_send()
    for buf, sems in (
        (gbuf, g_sem), (ss_row, sr_sem), (ss_col, sc_sem), (ss_sec, ss_sem),
    ):
        whole(buf, sems.at[0], sems.at[1], buf.shape[0] - 1).wait_send()


def scale_kernel(n_out, raw, factor_ref, gp_ref, gw_hbm, gp_hbm, out_buf, sems):
    gp_copy = pltpu.make_async_copy(gp_ref, gp_hbm, sems.at[n_out])
    gp_copy.start()
    factor = factor_ref[0:1, 0:1]
    size = raw.shape[0] // n_out
    copies = []
    for t in range(n_out):
        at = pl.ds(t * size, size)
        out_buf[at, :] = (raw[at, :] * factor).astype(jnp.bfloat16)
        c = pltpu.make_async_copy(out_buf.at[at, :], gw_hbm.at[0, at, :], sems.at[t])
        c.start()
        copies.append(c)
    for c in copies:
        c.wait()
    gp_copy.wait()


def on_device(sizes, grad_out, pre_act, w_down):
    n_sec, n_row, n_col = sizes
    f32, bf16 = jnp.float32, jnp.bfloat16
    _, hidden, feats = w_down.shape
    width = hidden + hidden // QUARTERS
    norm_target = target_rms * math.sqrt(float(n_sec * hidden * n_col * feats * n_row))
    dma = pltpu.SemaphoreType.DMA
    n_ag, n_rs = AG_PARTS * (n_row - 1), RS_PARTS * (n_row - 1) - n_row
    vmem = pl.BlockSpec(memory_space=pltpu.VMEM)
    hbm = pl.BlockSpec(memory_space=pl.ANY)
    small = (8, 128)
    gp, raw, factor = pl.pallas_call(
        functools.partial(kernel, n_row, n_col, n_sec, norm_target),
        out_shape=(
            pltpu.VMEM(pre_act.shape, bf16),
            pltpu.VMEM((hidden, feats), f32),
            pltpu.VMEM(small, f32),
        ),
        in_specs=[hbm, hbm, hbm],
        out_specs=(vmem, vmem, vmem),
        scratch_shapes=[
            pltpu.VMEM(grad_out.shape, bf16),
            pltpu.VMEM(pre_act.shape, bf16),
            pltpu.VMEM((hidden, feats), bf16),
            pltpu.VMEM((n_row, ROWS, width), bf16),
            pltpu.VMEM((ROWS, width), f32),
            pltpu.VMEM((ROWS, width), f32),
            pltpu.VMEM((n_col, 2, 2, ROWS, feats), bf16),
            pltpu.VMEM((n_row, ROWS, feats), bf16),
            pltpu.VMEM((n_row, ROWS, feats), bf16),
            pltpu.VMEM((n_row, ROWS, width), f32),
            pltpu.VMEM((n_row, ROWS, width // RS_PARTS + 128), bf16),
            pltpu.VMEM((n_row, ROWS, width // RS_PARTS + 128), bf16),
            pltpu.VMEM((n_rs, ROWS, width // RS_PARTS), bf16),
            pltpu.VMEM((n_rs, ROWS, width // RS_PARTS), bf16),
            pltpu.VMEM((1, ROWS, 128), f32),
            pltpu.VMEM((n_row,) + small, f32),
            pltpu.VMEM((n_col,) + small, f32),
            pltpu.VMEM((n_sec,) + small, f32),
            dma((2,)), dma, dma, dma((n_ag,)), dma, dma((n_row,)), dma, dma((n_rs,)),
            dma((2,)), dma((2,)), dma((2,)), dma((2,)),
        ],
        compiler_params=pltpu.CompilerParams(
            collective_id=0, has_side_effects=True, vmem_limit_bytes=58 * 1024 * 1024
        ),
        cost_estimate=pl.CostEstimate(
            flops=4 * 320 * hidden * feats, bytes_accessed=4 * hidden * feats, transcendentals=0
        ),
    )(grad_out, pre_act, w_down)
    n_out = 4
    gw, gp = pl.pallas_call(
        functools.partial(scale_kernel, n_out),
        out_shape=(
            jax.ShapeDtypeStruct(w_down.shape, bf16),
            jax.ShapeDtypeStruct(pre_act.shape, bf16),
        ),
        in_specs=[vmem, vmem, vmem],
        out_specs=(hbm, hbm),
        scratch_shapes=[pltpu.VMEM((hidden, feats), bf16), dma((n_out + 1,))],
        compiler_params=pltpu.CompilerParams(vmem_limit_bytes=16 * 1024 * 1024),
    )(raw, factor, gp)
    return gp, gw


def solution(mesh):
    sizes = (mesh.shape["section"], mesh.shape["row"], mesh.shape["col"])
    in_specs = (P("section", "col", "row"), P("section", "row", "col"), P("section", "col", "row"))
    out_specs = (P("section", "row", "col"), P("section", "col", "row"))
    return jax.shard_map(
        functools.partial(on_device, sizes), mesh=mesh, in_specs=in_specs, out_specs=out_specs,
        check_vma=False,
    )
```
